128 devices in a mesh: dp: 8 (over y_hi, x), tensor: 16 (over y_lo, z, core).
Axes of the slice: x: 4, y: 4 (y_hi: 2, y_lo: 2; y = y_hi * 2 + y_lo), z: 4, core: 2. Of those that a mesh axis runs over, the one named last changes fastest.
Arguments:
- inputs: bfloat16 [4096, 4096], P(('dp', 'tensor')), may hold values from -6 to 6
- out_grads: bfloat16 [4096, 4096], P(('dp', 'tensor')), may hold values from -6 to 6
- w_gate: bfloat16 [4096, 14784], P(None, 'tensor'), may hold values from -0.09375 to 0.09375
- w_up: bfloat16 [4096, 14784], P(None, 'tensor'), may hold values from -0.09375 to 0.09375
- w_down: bfloat16 [14784, 4096], P('tensor'), may hold values from -0.046875 to 0.046875
Outputs:
- in_grads: bfloat16 [4096, 4096], P(('dp', 'tensor'))
- g_gate: bfloat16 [4096, 14784], P('dp', 'tensor')
- g_up: bfloat16 [4096, 14784], P('dp', 'tensor')
- g_down: bfloat16 [14784, 4096], P('tensor', 'dp')
The draws below stay inside these ranges and needn't reach their ends.
All inputs are finite; a program needn't handle non-finite values.
Results may differ from the reference program's by a relative error of at most 0.023.
Values may be sent and summed in bfloat16 or wider, within the bound.
No kernel may reach another device: no remote copies, remote signals or barrier semaphores. Data moves between devices by JAX's collectives and lax.ppermute only.
A program may use at most 192 MiB of HBM per device.

```python
import jax
import jax.numpy as jnp
from jax import lax

D = 4096
FF = 14784
TOK = 512
TOKENS = 4096
N_DP = 8
N_TENSOR = 16


def block_scale(key, dims, cuts, smallest, high):
    factor_of, own = 1.0, jax.random.fold_in(key, 6)
    for dim, parts in cuts:
        steps = jnp.exp(jax.random.uniform(jax.random.fold_in(own, dim), (parts,), jnp.float32, smallest / len(cuts), high / len(cuts)))
        factor_of = factor_of * jnp.repeat(steps, dims[dim] // parts).reshape([-1 if axis == dim else 1 for axis in range(len(dims))])
    return factor_of


def scatter_about(rng, extent, scale, limit, cuts=(), held_as=jnp.bfloat16):
    level = block_scale(rng, extent, cuts, -0.22, 0.18) if cuts else 1.0
    entries = jax.random.normal(rng, extent, jnp.float32) * scale * level
    return jnp.minimum(jnp.maximum(entries, -limit), limit).astype(held_as)


def setup_inputs(seed: int = 0) -> dict:
    streams_of = jax.random.split(jax.random.key(seed), 6)
    inputs = scatter_about(streams_of[0], (TOKENS, D), 1.0, 6.0, ((0, 128),))
    out_grads = scatter_about(streams_of[1], (TOKENS, D), 1.0, 6.0, ((0, 128),))
    w_gate = scatter_about(streams_of[2], (D, FF), D ** -0.5, 0.09375, ((1, 16),))
    w_up = scatter_about(streams_of[3], (D, FF), D ** -0.5, 0.09375, ((1, 16),))
    w_down = scatter_about(streams_of[4], (FF, D), FF ** -0.5, 0.046875, ((0, 16),))
    return dict(inputs=inputs, out_grads=out_grads, w_gate=w_gate, w_up=w_up, w_down=w_down)


def contract_last(left, right):
    return lax.dot_general(left, right, (((1,), (1,)), ((), ())), preferred_element_type=jnp.float32)


def reference(inputs, out_grads, w_gate, w_up, w_down):
    shards = N_TENSOR
    local = FF // shards
    gate_wide = w_gate.astype(jnp.float32).reshape(D, shards, local)
    up_wide = w_up.astype(jnp.float32).reshape(D, shards, local)
    group_inputs = inputs.reshape(N_DP, TOK, D)
    group_grads = out_grads.reshape(N_DP, TOK, D)

    def rounded(value):
        return lax.optimization_barrier(value.astype(jnp.bfloat16)).astype(jnp.float32)

    def one_group(totals, pair):
        rows, grads = pair
        gate = jnp.dot(rows, w_gate, preferred_element_type=jnp.float32)
        up = jnp.dot(rows, w_up, preferred_element_type=jnp.float32)
        sig = jax.nn.sigmoid(gate)
        act = gate * sig
        hidden = (act * up).astype(jnp.bfloat16)
        d_hidden = contract_last(grads, w_down)
        d_up = (d_hidden * act).astype(jnp.bfloat16)
        d_gate = (d_hidden * up * sig * (1.0 + gate * (1.0 - sig))).astype(jnp.bfloat16)
        terms = jnp.einsum('tkf,dkf->ktd', d_gate.astype(jnp.float32).reshape(TOK, shards, local), gate_wide)
        terms = terms + jnp.einsum('tkf,dkf->ktd', d_up.astype(jnp.float32).reshape(TOK, shards, local), up_wide)
        in_rows = jnp.sum(rounded(terms), axis=0).astype(jnp.bfloat16)
        part_gate = rounded(jnp.dot(rows.T, d_gate, preferred_element_type=jnp.float32))
        part_up = rounded(jnp.dot(rows.T, d_up, preferred_element_type=jnp.float32))
        part_down = rounded(jnp.dot(hidden.T, grads, preferred_element_type=jnp.float32))
        return (totals[0] + part_gate, totals[1] + part_up, totals[2] + part_down), in_rows

    start = (jnp.zeros((D, FF), jnp.float32), jnp.zeros((D, FF), jnp.float32), jnp.zeros((FF, D), jnp.float32))
    totals, in_rows = lax.scan(one_group, start, (group_inputs, group_grads))
    in_grads = in_rows.reshape(N_DP * TOK, D)
    return (in_grads, totals[0].astype(jnp.bfloat16), totals[1].astype(jnp.bfloat16), totals[2].astype(jnp.bfloat16))
```

```python
import functools

import jax
import jax.numpy as jnp
from jax import lax
from jax.experimental import pallas as pl
from jax.experimental.pallas import tpu as pltpu
from jax.sharding import Mesh, PartitionSpec as P

D = 4096
FF = 924
TILE = 256
N_TILES = 4
LAST = 160
ROWS = 3 * (3 * TILE + LAST)
BF = jnp.bfloat16
F32 = jnp.float32
VMEM_LIMIT = 56 * 1024 * 1024


def ring(n, step):
    return [(i, (i + step) % n) for i in range(n)]


def send_x(a, step):
    return lax.ppermute(a, "x", ring(4, step))


def send_z(a, step):
    return lax.ppermute(a, "z", ring(4, step))


def swap(a, axis):
    return lax.ppermute(a, axis, [(0, 1), (1, 0)])


def dot(a, b, ca, cb):
    return lax.dot_general(a, b, (((ca,), (cb,)), ((), ())), preferred_element_type=F32)


def hidden_kernel(own_ref, other_ref, wg_ref, wu_ref, wd_ref, dt_ref, dn_ref, tok):
    j = pl.program_id(0)

    @pl.when(j == 0)
    def _():
        for a in range(2):
            tok[a, :128, :] = own_ref[a]
            tok[a, 128:, :] = other_ref[a]

    gate = dot(tok[0], wg_ref[...], 1, 0)
    up = dot(tok[0], wu_ref[...], 1, 0)
    d_hidden = dot(tok[1], wd_ref[...], 1, 1)
    sig = 1.0 / (1.0 + jnp.exp(-gate))
    act = gate * sig
    hidden = (act * up).astype(BF)
    d_up = (d_hidden * act).astype(BF)
    d_gate = (d_hidden * up * sig * (1.0 + gate * (1.0 - sig))).astype(BF)
    dn_ref[0] = d_gate
    dn_ref[1] = d_up
    gate_t, up_t, hidden_t = d_gate.T, d_up.T, hidden.T

    @pl.when(j < N_TILES - 1)
    def _():
        dt_ref[:TILE] = gate_t
        dt_ref[TILE : 2 * TILE] = up_t
        dt_ref[2 * TILE :] = hidden_t

    @pl.when(j == N_TILES - 1)
    def _():
        dt_ref[:LAST] = gate_t[:LAST]
        dt_ref[LAST : 2 * LAST] = up_t[:LAST]
        dt_ref[2 * LAST : 3 * LAST] = hidden_t[:LAST]


def hidden_call(own, other, w_gate, w_up, w_down):
    return pl.pallas_call(
        hidden_kernel,
        grid=(N_TILES,),
        in_specs=[
            pl.BlockSpec((2, 128, D), lambda j: (0, 0, 0)),
            pl.BlockSpec((2, 128, D), lambda j: (0, 0, 0)),
            pl.BlockSpec((D, TILE), lambda j: (0, j)),
            pl.BlockSpec((D, TILE), lambda j: (0, j)),
            pl.BlockSpec((TILE, D), lambda j: (j, 0)),
        ],
        out_specs=[
            pl.BlockSpec((3 * TILE, 256), lambda j: (j, 0)),
            pl.BlockSpec((2, 256, TILE), lambda j: (0, 0, j)),
        ],
        out_shape=[
            jax.ShapeDtypeStruct((ROWS, 256), BF),
            jax.ShapeDtypeStruct((2, 256, FF), BF),
        ],
        scratch_shapes=[pltpu.VMEM((2, 256, D), BF)],
        compiler_params=pltpu.CompilerParams(vmem_limit_bytes=VMEM_LIMIT),
        cost_estimate=pl.CostEstimate(
            flops=3 * 2 * 256 * D * FF, bytes_accessed=3 * 2 * D * FF, transcendentals=256 * FF
        ),
        name="hidden_grads",
    )(own, other, w_gate, w_up, w_down)


def in_grads_kernel(dn0_ref, dn1_ref, wg_ref, wu_ref, own_ref, other_ref):
    for b, dn_ref in enumerate((dn0_ref, dn1_ref)):
        p = dot(dn_ref[0], wg_ref[...], 1, 1) + dot(dn_ref[1], wu_ref[...], 1, 1)
        p = p.astype(BF)
        own_ref[b] = p[:128]
        other_ref[b] = p[128:]


def in_grads_call(dn0, dn1, w_gate, w_up):
    cols = 512
    whole = pl.BlockSpec((2, 256, FF), lambda j: (0, 0, 0))
    weight = pl.BlockSpec((cols, FF), lambda j: (j, 0))
    out = pl.BlockSpec((2, 128, cols), lambda j: (0, 0, j))
    return pl.pallas_call(
        in_grads_kernel,
        grid=(D // cols,),
        in_specs=[whole, whole, weight, weight],
        out_specs=[out, out],
        out_shape=[jax.ShapeDtypeStruct((2, 128, D), BF)] * 2,
        compiler_params=pltpu.CompilerParams(vmem_limit_bytes=VMEM_LIMIT),
        cost_estimate=pl.CostEstimate(
            flops=2 * 2 * 512 * D * FF, bytes_accessed=2 * 2 * D * FF, transcendentals=0
        ),
        name="in_grads_terms",
    )(dn0, dn1, w_gate, w_up)


def weights_kernel(n, pos_ref, *refs):
    pieces, x_ref, send_ref, keep_ref, stack = refs[:8], refs[8], refs[9], refs[10], refs[11]
    h = pl.program_id(0)
    yl = pos_ref[1]

    @pl.when(h == 0)
    def _():
        for b in range(2):
            for s in range(4):
                stack[b ^ yl, :, s * 256 : (s + 1) * 256] = pieces[b * 4 + s][: 3 * n]

    def total(rows, a):
        return (
            dot(stack[0, rows, :], x_ref[a, 0], 1, 0) + dot(stack[1, rows, :], x_ref[a, 1], 1, 0)
        ).astype(BF)

    def write(out_ref):
        out_ref[: 2 * n] = total(slice(0, 2 * n), 0)
        out_ref[2 * n :] = total(slice(2 * n, 3 * n), 1)

    @pl.when(h == 0)
    def _():
        write(send_ref)

    @pl.when(h == 1)
    def _():
        write(keep_ref)


def weights_call(n, pos, pieces, x_cols):
    specs = []
    for array, j in pieces:
        if j is None:
            specs.append(pl.BlockSpec((3 * n, 256), lambda h, p: (0, 0)))
        else:
            specs.append(pl.BlockSpec((3 * TILE, 256), functools.partial(lambda j, h, p: (j, 0), j)))
    specs.append(
        pl.BlockSpec((2, 2, 1024, 512), lambda h, p: (0, 0, 0, (p[0] + 1 + h) % 2))
    )
    out = pl.BlockSpec((3 * n, 512), lambda h, p: (0, 0))
    return pl.pallas_call(
        functools.partial(weights_kernel, n),
        grid_spec=pltpu.PrefetchScalarGridSpec(
            num_scalar_prefetch=1,
            grid=(2,),
            in_specs=specs,
            out_specs=[out, out],
            scratch_shapes=[pltpu.VMEM((2, 3 * n, 1024), BF)],
        ),
        out_shape=[jax.ShapeDtypeStruct((3 * n, 512), BF)] * 2,
        compiler_params=pltpu.CompilerParams(vmem_limit_bytes=VMEM_LIMIT),
        cost_estimate=pl.CostEstimate(
            flops=2 * 3 * n * 2048 * 1024, bytes_accessed=8 * 1024 * 1024, transcendentals=0
        ),
        name="weight_grads",
    )(pos, *[a for a, _ in pieces], x_cols)


def natural(pieces, index, n):
    return [lax.select_n((k - index) % n, *pieces) for k in range(n)]


def on_device(inputs, out_grads, w_gate, w_up, w_down):
    xi, yh, yl, zi = (lax.axis_index(a) for a in ("x", "yh", "yl", "z"))
    pos = jnp.stack([yh, yl]).astype(jnp.int32)
    mine = jnp.stack([inputs, out_grads])

    cols = mine.reshape(2, 32, 2, 4, 512)

    def block_for(step):
        return lax.dynamic_index_in_dim(cols, (xi + step) % 4, axis=3, keepdims=False).reshape(2, 32, 1024)

    from_x = [block_for(0), send_x(block_for(1), 1), send_x(block_for(3), -1), send_x(block_for(2), 2)]
    shares = jnp.stack(from_x, axis=1)
    own_cols = lax.all_gather(shares, ("yl", "z"), axis=0, tiled=False)
    other_cols = swap(own_cols, "core")
    x_cols = jnp.stack([own_cols, other_cols]).reshape(2, 2, 4, 2, 4, 32, 1024)
    x_cols = x_cols.transpose(3, 1, 4, 0, 2, 5, 6).reshape(2, 2, 1024, 1024)

    def gather_z(piece):
        right, left = send_z(piece, 1), send_z(piece, -1)
        far = jnp.stack([send_z(right[0], 1), send_z(left[1], -1)])
        whole = jnp.stack(natural([piece, left, far, right], zi, 4), axis=1)
        return whole.reshape(2, 128, D)

    partner = swap(mine, "yl")
    batch0 = gather_z(mine)
    dt0, dn0 = hidden_call(batch0, swap(batch0, "core"), w_gate, w_up, w_down)
    batch1 = gather_z(partner)
    dt1, dn1 = hidden_call(batch1, swap(batch1, "core"), w_gate, w_up, w_down)

    term_own, term_other = in_grads_call(dn0, dn1, w_gate, w_up)
    pair = (term_own.astype(F32) + swap(term_other, "core").astype(F32)).astype(BF)
    pair = jnp.stack(natural([pair[0], pair[1]], yl, 2))
    in_grads = lax.psum_scatter(pair.reshape(256, D), ("yl", "z"), scatter_dimension=0, tiled=True)

    right0, left0 = send_x(dt0, 1), send_x(dt0, -1)
    kept, sent = [], []
    for j in range(N_TILES):
        n = TILE if j < N_TILES - 1 else LAST
        rows = slice(3 * TILE * j, 3 * TILE * j + 3 * n)
        far0 = send_x(right0[rows], 1)
        right1, left1 = send_x(dt1[rows], 1), send_x(dt1[rows], -1)
        far1 = send_x(left1, -1)
        pieces = [
            (dt0, j), (right0, j), (left0, j), (far0, None),
            (dt1, j), (right1, None), (left1, None), (far1, None),
        ]
        send, keep = weights_call(n, pos, pieces, x_cols)
        kept.append(keep)
        sent.append(swap(send, "yh"))

    gate_parts, up_parts, down_parts = [], [], []
    for j in range(N_TILES):
        n = TILE if j < N_TILES - 1 else LAST
        used = min(n, FF - TILE * j)
        total = (kept[j].astype(F32) + sent[j].astype(F32)).astype(BF)
        gate_parts.append(total[:used])
        up_parts.append(total[n : n + used])
        down_parts.append(total[2 * n : 2 * n + used])
    g_gate = jnp.concatenate(gate_parts, axis=0).T
    g_up = jnp.concatenate(up_parts, axis=0).T
    g_down = jnp.concatenate(down_parts, axis=0)
    return in_grads, g_gate, g_up, g_down


def solution(mesh):
    fine = Mesh(mesh.devices.reshape(2, 4, 2, 4, 2), ("yh", "x", "yl", "z", "core"))
    tokens = P(("yh", "x", "yl", "z", "core"), None)
    units = ("yl", "z", "core")
    groups = ("yh", "x")
    return jax.shard_map(
        on_device,
        mesh=fine,
        in_specs=(tokens, tokens, P(None, units), P(None, units), P(units, None)),
        out_specs=(tokens, P(groups, units), P(groups, units), P(units, groups)),
        check_vma=False,
    )
```

```python
import functools

import jax
import jax.numpy as jnp
from jax import lax
from jax.experimental import pallas as pl
from jax.experimental.pallas import tpu as pltpu
from jax.sharding import Mesh, PartitionSpec as P

D = 4096
FF = 924
TILE = 256
N_TILES = 4
LAST = 160
ROWS = 3 * (3 * TILE + LAST)
BF = jnp.bfloat16
F32 = jnp.float32
VMEM_LIMIT = 48 * 1024 * 1024
ANY = pl.BlockSpec(memory_space=pl.ANY)
COST = 8


ORDER = (((0, 0), (0, 1), (0, 3), (1, 0)), ((0, 2), (1, 2), (1, 1), (1, 3)))
SLOT = {step: (b, k) for b in range(2) for k, step in enumerate(ORDER[b])}


def ring(n, step):
    return [(i, (i + step) % n) for i in range(n)]


def send_x(a, step):
    return lax.ppermute(a, "x", ring(4, step))


def send_z(a, step):
    return lax.ppermute(a, "z", ring(4, step))


def swap(a, axis):
    return lax.ppermute(a, axis, [(0, 1), (1, 0)])


def dot(a, b, ca, cb):
    return lax.dot_general(a, b, (((ca,), (cb,)), ((), ())), preferred_element_type=F32)


def after(a, *others):
    return lax.optimization_barrier((a, *others))[0]


def hidden_kernel(places, *refs):
    pieces, (wg_ref, wu_ref, wd_ref, dt_ref, dn_ref, tok, sems) = refs[:-7], refs[-7:]
    j = pl.program_id(0)

    @pl.when(j == 0)
    def _():
        copies = []

        def put(src, dst):
            copies.append(pltpu.make_async_copy(src, dst, sems.at[len(copies)]))

        for c in range(2):
            for i, place in enumerate(places):
                ref = pieces[len(places) * c + i]
                for part, (array, k) in enumerate(place):
                    dst = pl.ds(128 * c + 32 * k, 32)
                    if array is None:
                        put(ref, tok.at[:, dst, :])
                    else:
                        put(ref.at[part], tok.at[array, dst, :])
        for copy in copies:
            copy.start()
        for copy in copies:
            copy.wait()

    gate = dot(wg_ref[...], tok[0], 1, 1)
    up = dot(wu_ref[...], tok[0], 1, 1)
    d_hidden = dot(wd_ref[...], tok[1], 1, 1)
    sig = 1.0 / (1.0 + jnp.exp(-gate))
    act = gate * sig
    hidden = (act * up).astype(BF)
    d_up = (d_hidden * act).astype(BF)
    d_gate = (d_hidden * up * sig * (1.0 + gate * (1.0 - sig))).astype(BF)
    dn_ref[0] = d_gate.T
    dn_ref[1] = d_up.T

    @pl.when(j < N_TILES - 1)
    def _():
        dt_ref[:TILE] = d_gate
        dt_ref[TILE : 2 * TILE] = d_up
        dt_ref[2 * TILE :] = hidden

    @pl.when(j == N_TILES - 1)
    def _():
        dt_ref[:LAST] = d_gate[:LAST]
        dt_ref[LAST : 2 * LAST] = d_up[:LAST]
        dt_ref[2 * LAST : 3 * LAST] = hidden[:LAST]


def hidden_call(pieces, places, wg_rows, wu_rows, w_down):
    weight = pl.BlockSpec((TILE, D), lambda j: (j, 0))
    return pl.pallas_call(
        functools.partial(hidden_kernel, places),
        grid=(N_TILES,),
        in_specs=[ANY] * len(pieces) + [weight] * 3,
        out_specs=[
            pl.BlockSpec((3 * TILE, 256), lambda j: (j, 0)),
            pl.BlockSpec((2, 256, TILE), lambda j: (0, 0, j)),
        ],
        out_shape=[
            jax.ShapeDtypeStruct((ROWS, 256), BF),
            jax.ShapeDtypeStruct((2, 256, FF), BF),
        ],
        scratch_shapes=[pltpu.VMEM((2, 256, D), BF), pltpu.SemaphoreType.DMA((16,))],
        compiler_params=pltpu.CompilerParams(vmem_limit_bytes=VMEM_LIMIT),
        cost_estimate=pl.CostEstimate(
            flops=6 * 256 * D * FF // COST, bytes_accessed=6 * D * FF // COST, transcendentals=0
        ),
        name="hidden_grads",
    )(*pieces, wg_rows, wu_rows, w_down)


def in_grads_kernel(pos_ref, dn0_ref, dn1_ref, wg_ref, wu_ref, own_ref, other_ref, dn):
    @pl.when(pl.program_id(0) == 0)
    def _():
        for a in range(2):
            dn[a, :256, :] = dn0_ref[a]
            dn[a, 256:, :] = dn1_ref[a]

    p = (dot(dn[0], wg_ref[...], 1, 0) + dot(dn[1], wu_ref[...], 1, 0)).astype(BF)
    yl, z = pos_ref[0], pos_ref[1]
    for b in range(2):
        for c, out_ref in enumerate((own_ref, other_ref)):
            for i, (y_step, z_step) in enumerate(ORDER[b]):
                row = 256 * b + 128 * c + 32 * i
                out_ref[y_step ^ yl, lax.rem(z_step + z, 4)] = p[row : row + 32]


def in_grads_call(pos, dn0, dn1, wg_rows, wu_rows):
    cols = 512
    whole = pl.BlockSpec((2, 256, FF), lambda j, p: (0, 0, 0))
    weight = pl.BlockSpec((FF, cols), lambda j, p: (0, j))
    out = pl.BlockSpec((2, 4, 32, cols), lambda j, p: (0, 0, 0, j))
    return pl.pallas_call(
        in_grads_kernel,
        grid_spec=pltpu.PrefetchScalarGridSpec(
            num_scalar_prefetch=1,
            grid=(D // cols,),
            in_specs=[whole, whole, weight, weight],
            out_specs=[out, out],
            scratch_shapes=[pltpu.VMEM((2, 512, FF), BF)],
        ),
        out_shape=[jax.ShapeDtypeStruct((2, 4, 32, D), BF)] * 2,
        compiler_params=pltpu.CompilerParams(vmem_limit_bytes=VMEM_LIMIT),
        cost_estimate=pl.CostEstimate(
            flops=4 * 512 * D * FF // COST, bytes_accessed=4 * D * FF // COST, transcendentals=0
        ),
        name="in_grads_terms",
    )(pos, dn0, dn1, wg_rows, wu_rows)


def weights_kernel(n, starts, *refs):
    pieces, col_pieces = refs[:8], refs[8:18]
    send_ref, keep_ref, stack, x, sems = refs[18:]
    halves = ([], [])
    count = [0]

    def put(group, src, dst):
        copy = pltpu.make_async_copy(src, dst, sems.at[count[0]])
        count[0] += 1
        copy.start()
        group.append(copy)

    for b in range(2):
        for s in range(4):
            i = 4 * b + s
            put(
                halves[0],
                pieces[i].at[pl.ds(starts[i], 3 * n), :],
                stack.at[b, :, pl.ds(256 * s, 256)],
            )
    for h in range(2):
        cols = pl.ds(512 * h, 512)
        for c in range(2):
            here, left, far_in, far_grad, right = col_pieces[5 * c : 5 * c + 5]
            for y in range(2):
                for z, ref in ((0, here), (1, left), (3, right)):
                    b, k = SLOT[y, z]
                    put(halves[h], ref.at[y, :, :, :, cols], x.at[b, :, :, c, k, :, cols])
                b, k = SLOT[y, 2]
                put(halves[h], far_in.at[y, :, :, cols], x.at[b, 0, :, c, k, :, cols])
                put(halves[h], far_grad.at[y, :, :, cols], x.at[b, 1, :, c, k, :, cols])

    for h, out_ref in enumerate((send_ref, keep_ref)):
        for copy in halves[h]:
            copy.wait()

        def total(rows, a):
            parts = [
                dot(stack[b, rows, :], x[b, a, :, :, :, :, 512 * h : 512 * h + 512].reshape(1024, 512), 1, 0)
                for b in range(2)
            ]
            return (parts[0] + parts[1]).astype(BF)

        out_ref[: 2 * n] = total(slice(0, 2 * n), 0)
        out_ref[2 * n :] = total(slice(2 * n, 3 * n), 1)


def weights_call(n, pieces, col_pieces):
    return pl.pallas_call(
        functools.partial(weights_kernel, n, [s for _, s in pieces]),
        in_specs=[ANY] * 18,
        out_specs=[pl.BlockSpec(memory_space=pltpu.VMEM)] * 2,
        out_shape=[jax.ShapeDtypeStruct((3 * n, 512), BF)] * 2,
        scratch_shapes=[
            pltpu.VMEM((2, 3 * n, 1024), BF),
            pltpu.VMEM((2, 2, 4, 2, 4, 32, 1024), BF),
            pltpu.SemaphoreType.DMA((48,)),
        ],
        compiler_params=pltpu.CompilerParams(vmem_limit_bytes=VMEM_LIMIT),
        cost_estimate=pl.CostEstimate(
            flops=6 * n * 2048 * 1024 // COST, bytes_accessed=(12 << 20) // COST, transcendentals=0
        ),
        name="weight_grads",
    )(*[a for a, _ in pieces], *col_pieces)


def gate(*arrays):
    return lax.optimization_barrier(arrays)


def core_swaps(pieces):
    return [swap(p, "core") for p in pieces]


def on_device(inputs, out_grads, w_gate, w_up, w_down):
    xi, yh, yl, zi = (lax.axis_index(a) for a in ("x", "yh", "yl", "z"))
    pos = jnp.stack([yl, zi]).astype(jnp.int32)
    wg_rows, wu_rows = w_gate.T, w_up.T
    mine = jnp.stack([inputs, out_grads])

    def block_for(step):
        group = lax.rem(xi + step, 4)
        starts = [((1 - yh) * 4 + group) * 512, (yh * 4 + group) * 512]
        return jnp.concatenate([lax.dynamic_slice_in_dim(mine, s, 512, axis=2) for s in starts], axis=2)

    right, left = send_z(mine, 1), send_z(mine, -1)
    partner = swap(mine, "yl")
    from_x = [block_for(0), send_x(block_for(1), 1), send_x(block_for(3), -1), send_x(block_for(2), 2)]
    right, left, partner, *from_x = gate(right, left, partner, *from_x)

    shares = jnp.stack(from_x, axis=1)
    other_shares = swap(shares, "yl")
    p_right, p_left = send_z(partner, 1), send_z(partner, -1)
    batch0 = [mine, left, right, partner]
    batch0 += core_swaps(batch0)
    both = ((None, 0),), ((None, 1),), ((None, 2),), ((None, 3),)
    dt0, dn0 = hidden_call(batch0, both, wg_rows, wu_rows, w_down)
    dt0, dn0, p_right, p_left, shares, other_shares = gate(dt0, dn0, p_right, p_left, shares, other_shares)

    lanes = {1: [], -1: []}

    def in_turn(a, step):
        lane = lanes[step]
        if len(lane) >= 2:
            a = after(a, lane[-2])
        lane.append(send_x(a, step))
        return lane[-1]

    right0, left0 = in_turn(dt0, 1), in_turn(dt0, -1)
    far_in = send_z(jnp.stack([right[0], p_right[0]]), 1)
    far_grad = send_z(jnp.stack([left[1], p_left[1]]), -1)
    batch1 = [far_in, far_grad, p_left, p_right]
    batch1 += core_swaps(batch1)
    shares = jnp.stack([shares, other_shares])
    shares, *batch1 = gate(shares, *batch1)

    places = ((0, 0), (0, 1)), ((1, 0), (1, 1)), ((None, 2),), ((None, 3),)
    dt1, dn1 = hidden_call(batch1, places, wg_rows, wu_rows, w_down)
    c_right, c_left = send_z(shares, 1), send_z(shares, -1)
    dt1, dn1, c_right, c_left, right0, left0 = gate(dt1, dn1, c_right, c_left, right0, left0)

    term_own, term_other = in_grads_call(pos, dn0, dn1, wg_rows, wu_rows)
    col_pieces = [shares, c_left, send_z(c_right[:, 0], 1), send_z(c_left[:, 1], -1), c_right]
    col_pieces += core_swaps(col_pieces)

    kept, sent = [], []
    for j in range(N_TILES):
        n = TILE if j < N_TILES - 1 else LAST
        start = 3 * TILE * j
        rows = slice(start, start + 3 * n)
        right0_rows, dt1_rows = right0[rows], dt1[rows]
        if j == 1:
            term_own, term_other, right0_rows, dt1_rows = gate(term_own, term_other, right0_rows, dt1_rows)
        if j >= 2:
            send, keep, right0_rows, dt1_rows = gate(sent[j - 2], kept[j - 2], right0_rows, dt1_rows)
            sent[j - 2], kept[j - 2] = send, keep
        far0, left1 = in_turn(right0_rows, 1), in_turn(dt1_rows, -1)
        right1, far1 = in_turn(dt1_rows, 1), in_turn(left1, -1)
        pieces = [
            (dt0, start), (right0, start), (left0, start), (far0, 0),
            (dt1, start), (right1, 0), (left1, 0), (far1, 0),
        ]
        send, keep = weights_call(n, pieces, col_pieces)
        kept.append(keep)
        sent.append(send)

    sent = [swap(a, "yh") for a in sent]
    pair = (term_own.astype(F32) + swap(term_other, "core").astype(F32)).astype(BF)
    in_grads = lax.psum_scatter(pair.reshape(256, D), ("yl", "z"), scatter_dimension=0, tiled=True)

    gate_parts, up_parts, down_parts = [], [], []
    for j in range(N_TILES):
        n = TILE if j < N_TILES - 1 else LAST
        used = min(n, FF - TILE * j)
        total = (kept[j].astype(F32) + sent[j].astype(F32)).astype(BF)
        gate_parts.append(total[:used])
        up_parts.append(total[n : n + used])
        down_parts.append(total[2 * n : 2 * n + used])
    g_gate = jnp.concatenate(gate_parts, axis=0).T
    g_up = jnp.concatenate(up_parts, axis=0).T
    g_down = jnp.concatenate(down_parts, axis=0)
    return in_grads, g_gate, g_up, g_down


def solution(mesh):
    fine = Mesh(mesh.devices.reshape(2, 4, 2, 4, 2), ("yh", "x", "yl", "z", "core"))
    tokens = P(("yh", "x", "yl", "z", "core"), None)
    units = ("yl", "z", "core")
    groups = ("yh", "x")
    return jax.shard_map(
        on_device,
        mesh=fine,
        in_specs=(tokens, tokens, P(None, units), P(None, units), P(units, None)),
        out_specs=(tokens, P(groups, units), P(groups, units), P(units, groups)),
        check_vma=False,
    )
```

```python
import functools

import jax
import jax.numpy as jnp
from jax import lax
from jax.experimental import pallas as pl
from jax.experimental.pallas import tpu as pltpu
from jax.sharding import Mesh, PartitionSpec as P

D = 4096
FF = 924
TILE = 256
N_TILES = 4
LAST = 160
UNITS = (TILE, TILE, TILE, LAST)
BF = jnp.bfloat16
F32 = jnp.float32
MIB = 1024 * 1024
ANY = pl.BlockSpec(memory_space=pl.ANY)
COST = 8


ORDER = (((0, 0), (0, 1), (0, 3), (1, 0)), ((0, 2), (1, 2), (1, 1), (1, 3)))
SOURCES = (0, 3, 1, 2)
SLOT = {step: (b, k) for b in range(2) for k, step in enumerate(ORDER[b])}


def ring(n, step):
    return [(i, (i + step) % n) for i in range(n)]


def send_x(a, step):
    return lax.ppermute(a, "x", ring(4, step))


def send_z(a, step):
    return lax.ppermute(a, "z", ring(4, step))


def swap(a, axis):
    return lax.ppermute(a, axis, [(0, 1), (1, 0)])


def dot(a, b, ca, cb):
    return lax.dot_general(a, b, (((ca,), (cb,)), ((), ())), preferred_element_type=F32)


def hidden_kernel(places, outs, *refs):
    n = len(outs)
    pieces, (wg_ref, wu_ref, wd_ref), dt_refs, (dn_ref, tok, sems) = (
        refs[: -6 - n],
        refs[-6 - n : -3 - n],
        refs[-3 - n : -3],
        refs[-3:],
    )
    j = pl.program_id(0)

    @pl.when(j == 0)
    def _():
        copies = []

        def put(src, dst):
            copies.append(pltpu.make_async_copy(src, dst, sems.at[len(copies)]))

        for c in range(2):
            for i, place in enumerate(places):
                ref = pieces[len(places) * c + i]
                for part, (array, k) in enumerate(place):
                    dst = pl.ds(128 * c + 32 * k, 32)
                    if array is None:
                        put(ref, tok.at[:, dst, :])
                    else:
                        put(ref.at[part], tok.at[array, dst, :])
        for copy in copies:
            copy.start()
        for copy in copies:
            copy.wait()

    gate = dot(wg_ref[...], tok[0], 1, 1)
    up = dot(wu_ref[...], tok[0], 1, 1)
    d_hidden = dot(wd_ref[...], tok[1], 1, 1)
    sig = 1.0 / (1.0 + jnp.exp(-gate))
    act = gate * sig
    hidden = (act * up).astype(BF)
    d_up = (d_hidden * act).astype(BF)
    d_gate = (d_hidden * up * sig * (1.0 + gate * (1.0 - sig))).astype(BF)
    dn_ref[0] = d_gate.T
    dn_ref[1] = d_up.T

    for dt_ref, tiles in zip(dt_refs, outs):
        for i, tile in enumerate(tiles):

            @pl.when(j == tile)
            def _():
                n = UNITS[tile]
                for part, value in enumerate((d_gate, d_up, hidden)):
                    row = 3 * TILE * i + n * part
                    dt_ref[row : row + n] = value[:n]


def hidden_call(pieces, places, outs, wg_rows, wu_rows, w_down):
    rows = [sum(3 * UNITS[t] for t in tiles) for tiles in outs]
    weight = pl.BlockSpec((TILE, D), lambda j: (j, 0))
    return pl.pallas_call(
        functools.partial(hidden_kernel, places, outs),
        grid=(N_TILES,),
        in_specs=[ANY] * len(pieces) + [weight] * 3,
        out_specs=[
            *[pl.BlockSpec((r, 256), lambda j: (0, 0)) for r in rows],
            pl.BlockSpec((2, 256, TILE), lambda j: (0, 0, j)),
        ],
        out_shape=[
            *[jax.ShapeDtypeStruct((r, 256), BF) for r in rows],
            jax.ShapeDtypeStruct((2, 256, FF), BF),
        ],
        scratch_shapes=[pltpu.VMEM((2, 256, D), BF), pltpu.SemaphoreType.DMA((16,))],
        compiler_params=pltpu.CompilerParams(vmem_limit_bytes=48 * MIB),
        cost_estimate=pl.CostEstimate(
            flops=6 * 256 * D * FF // COST, bytes_accessed=6 * D * FF // COST, transcendentals=0
        ),
        name="hidden_grads",
    )(*pieces, wg_rows, wu_rows, w_down)


def in_grads_kernel(pos_ref, dn0_ref, dn1_ref, wg_ref, wu_ref, own_ref, other_ref, dn):
    @pl.when(pl.program_id(0) == 0)
    def _():
        for a in range(2):
            dn[a, :256, :] = dn0_ref[a]
            dn[a, 256:, :] = dn1_ref[a]

    p = (dot(dn[0], wg_ref[...], 1, 0) + dot(dn[1], wu_ref[...], 1, 0)).astype(BF)
    yl, z = pos_ref[0], pos_ref[1]
    for b in range(2):
        for c, out_ref in enumerate((own_ref, other_ref)):
            for i, (y_step, z_step) in enumerate(ORDER[b]):
                row = 256 * b + 128 * c + 32 * i
                out_ref[lax.rem(z_step + z, 4), y_step ^ yl] = p[row : row + 32]


def in_grads_call(pos, dn0, dn1, wg_rows, wu_rows):
    cols = 512
    whole = pl.BlockSpec((2, 256, FF), lambda j, p: (0, 0, 0))
    weight = pl.BlockSpec((FF, cols), lambda j, p: (0, j))
    out = pl.BlockSpec((4, 2, 32, cols), lambda j, p: (0, 0, 0, j))
    return pl.pallas_call(
        in_grads_kernel,
        grid_spec=pltpu.PrefetchScalarGridSpec(
            num_scalar_prefetch=1,
            grid=(D // cols,),
            in_specs=[whole, whole, weight, weight],
            out_specs=[out, out],
            scratch_shapes=[pltpu.VMEM((2, 512, FF), BF)],
        ),
        out_shape=[jax.ShapeDtypeStruct((4, 2, 32, D), BF)] * 2,
        compiler_params=pltpu.CompilerParams(vmem_limit_bytes=48 * MIB),
        cost_estimate=pl.CostEstimate(
            flops=4 * 512 * D * FF // COST, bytes_accessed=4 * D * FF // COST, transcendentals=0
        ),
        name="in_grads_terms",
    )(pos, dn0, dn1, wg_rows, wu_rows)


def weights_kernel(n, places, pos_ref, *refs):
    pieces, col_pieces = refs[:5], refs[5:15]
    send_ref, keep_ref, stack, x, sems = refs[15:]
    start, stride, second = places
    sources = []
    for step in SOURCES:
        first = lax.rem(pos_ref[2] + step, 4) * stride + start
        sources.append(pieces[0].at[pl.ds(pl.multiple_of(first, 32), 3 * n), :])
    sources += [ref.at[pl.ds(second, 3 * n), :] for ref in pieces[1:4]]
    sources.append(pieces[4])
    halves = ([], [])
    count = [0]

    def put(group, src, dst):
        copy = pltpu.make_async_copy(src, dst, sems.at[count[0]])
        count[0] += 1
        copy.start()
        group.append(copy)

    for b in range(2):
        for s in range(4):
            i = 4 * b + s
            put(halves[0], sources[i], stack.at[b, :, pl.ds(256 * s, 256)])
    for h in range(2):
        cols = pl.ds(512 * h, 512)
        for c in range(2):
            here, left, far_in, far_grad, right = col_pieces[5 * c : 5 * c + 5]
            for y in range(2):
                for z, ref in ((0, here), (1, left), (3, right)):
                    b, k = SLOT[y, z]
                    put(halves[h], ref.at[y, :, :, :, cols], x.at[b, :, :, c, k, :, cols])
                b, k = SLOT[y, 2]
                put(halves[h], far_in.at[y, :, :, cols], x.at[b, 0, :, c, k, :, cols])
                put(halves[h], far_grad.at[y, :, :, cols], x.at[b, 1, :, c, k, :, cols])

    for h, out_ref in enumerate((send_ref, keep_ref)):
        for copy in halves[h]:
            copy.wait()

        def total(rows, a):
            parts = [
                dot(stack[b, rows, :], x[b, a, :, :, :, :, 512 * h : 512 * h + 512].reshape(1024, 512), 1, 0)
                for b in range(2)
            ]
            return (parts[0] + parts[1]).astype(BF)

        out_ref[: 2 * n] = total(slice(0, 2 * n), 0)
        out_ref[2 * n :] = total(slice(2 * n, 3 * n), 1)


def weights_call(n, pos, places, pieces, col_pieces):
    return pl.pallas_call(
        functools.partial(weights_kernel, n, places),
        in_specs=[pl.BlockSpec(memory_space=pltpu.SMEM)] + [ANY] * 15,
        out_specs=[pl.BlockSpec(memory_space=pltpu.VMEM)] * 2,
        out_shape=[jax.ShapeDtypeStruct((3 * n, 512), BF)] * 2,
        scratch_shapes=[
            pltpu.VMEM((2, 3 * n, 1024), BF),
            pltpu.VMEM((2, 2, 4, 2, 4, 32, 1024), BF),
            pltpu.SemaphoreType.DMA((48,)),
        ],
        compiler_params=pltpu.CompilerParams(vmem_limit_bytes=48 * MIB),
        cost_estimate=pl.CostEstimate(
            flops=6 * n * 2048 * 1024 // COST, bytes_accessed=(12 << 20) // COST, transcendentals=0
        ),
        name="weight_grads",
    )(pos, *pieces, *col_pieces)


def gate(*arrays):
    return lax.optimization_barrier(arrays)


def core_swaps(pieces):
    return [swap(p, "core") for p in pieces]


def on_device(inputs, out_grads, w_gate, w_up, w_down):
    xi, yh, yl, zi = (lax.axis_index(a) for a in ("x", "yh", "yl", "z"))
    pos = jnp.stack([yl, zi, xi]).astype(jnp.int32)
    wg_rows, wu_rows = w_gate.T, w_up.T
    mine = jnp.stack([inputs, out_grads])

    def block_for(step):
        group = lax.rem(xi + step, 4)
        starts = [((1 - yh) * 4 + group) * 512, (yh * 4 + group) * 512]
        return jnp.concatenate([lax.dynamic_slice_in_dim(mine, s, 512, axis=2) for s in starts], axis=2)

    right, left = send_z(mine, 1), send_z(mine, -1)
    partner = swap(mine, "yl")
    from_x = [block_for(0), send_x(block_for(1), 1), send_x(block_for(3), -1), send_x(block_for(2), 2)]
    right, left, partner, *from_x = gate(right, left, partner, *from_x)

    shares = jnp.stack(from_x, axis=1)
    other_shares = swap(shares, "yl")
    p_right, p_left = send_z(partner, 1), send_z(partner, -1)
    batch0 = [mine, left, right, partner]
    batch0 += core_swaps(batch0)
    both = ((None, 0),), ((None, 1),), ((None, 2),), ((None, 3),)
    own0, dn0 = hidden_call(batch0, both, ((0, 1, 2, 3),), wg_rows, wu_rows, w_down)
    own0, dn0, p_right, p_left, shares, other_shares = gate(own0, dn0, p_right, p_left, shares, other_shares)
    gathered0 = lax.all_gather(own0, "x", axis=0, tiled=True)

    far_in = send_z(jnp.stack([right[0], p_right[0]]), 1)
    far_grad = send_z(jnp.stack([left[1], p_left[1]]), -1)
    batch1 = [far_in, far_grad, p_left, p_right]
    batch1 += core_swaps(batch1)
    shares = jnp.stack([shares, other_shares])
    shares, *batch1 = gate(shares, *batch1)

    places = ((0, 0), (0, 1)), ((1, 0), (1, 1)), ((None, 2),), ((None, 3),)
    *own1, dn1 = hidden_call(batch1, places, ((0, 1), (2, 3)), wg_rows, wu_rows, w_down)
    c_right, c_left = send_z(shares, 1), send_z(shares, -1)
    right1, left1 = [send_x(own1[0], 1)], [send_x(own1[0], -1)]
    cut = 3 * TILE
    c_far_in, c_far_grad = send_z(c_right[:, 0], 1), send_z(c_left[:, 1], -1)
    shares_other = swap(shares, "core")
    term_own, term_other = in_grads_call(pos, dn0, dn1, wg_rows, wu_rows)
    term_own, term_other, c_far_in, c_far_grad, right1[0], left1[0], own1[1], shares_other, c_left, c_right, gathered0 = gate(
        term_own, term_other, c_far_in, c_far_grad, right1[0], left1[0], own1[1], shares_other, c_left, c_right, gathered0
    )

    far1 = [send_x(right1[0][:cut], 1), send_x(left1[0][cut:], -1)]
    c_here = [c_left, c_far_in, c_far_grad, c_right]
    c_other = core_swaps(c_here)
    term_other = swap(term_other, "core")
    *far1, own1[1], term_other = gate(*far1, own1[1], term_other, *c_other)[:4]
    col_pieces = [shares, *c_here, shares_other, *c_other]
    kept, sent, got = [], [], []

    def weights(j):
        side, start = j // 2, cut * (j % 2)
        pieces = [gathered0, own1[side], right1[side], left1[side], far1[j]]
        send, keep = weights_call(UNITS[j], pos, (cut * j, own0.shape[0], start), pieces, col_pieces)
        kept.append(keep)
        sent.append(send)

    right1.append(send_x(own1[1], 1))
    left1.append(send_x(own1[1], -1))
    weights(0)
    sent[0], own1[0], term_other = gate(sent[0], own1[0], term_other)
    pair = (term_own.astype(F32) + term_other.astype(F32)).astype(BF)
    scattered = lax.psum_scatter(pair.reshape(256, D), "z", scatter_dimension=0, tiled=True)
    got.append(swap(sent[0], "yh"))
    weights(1)
    right1[1], left1[1], sent[1] = gate(right1[1], left1[1], sent[1])
    got.append(swap(sent[1], "yh"))
    far1 += [send_x(right1[1][:cut], 1), send_x(left1[1][cut:], -1)]
    scattered = scattered.reshape(2, 32, D)
    mine_part = lax.dynamic_index_in_dim(scattered, yl, axis=0, keepdims=False)
    other_part = lax.dynamic_index_in_dim(scattered, 1 - yl, axis=0, keepdims=False)
    in_grads = (mine_part.astype(F32) + swap(other_part, "yl").astype(F32)).astype(BF)
    far1[2], far1[3], got[0], own1[1] = gate(far1[2], far1[3], got[0], own1[1])
    weights(2)
    got.append(swap(sent[2], "yh"))
    got[1], sent[2], own1[1] = gate(got[1], sent[2], own1[1])
    weights(3)
    got.append(swap(sent[3], "yh"))
    sent = got

    gate_parts, up_parts, down_parts = [], [], []
    for j in range(N_TILES):
        n = TILE if j < N_TILES - 1 else LAST
        used = min(n, FF - TILE * j)
        total = (kept[j].astype(F32) + sent[j].astype(F32)).astype(BF)
        gate_parts.append(total[:used])
        up_parts.append(total[n : n + used])
        down_parts.append(total[2 * n : 2 * n + used])
    g_gate = jnp.concatenate(gate_parts, axis=0).T
    g_up = jnp.concatenate(up_parts, axis=0).T
    g_down = jnp.concatenate(down_parts, axis=0)
    return in_grads, g_gate, g_up, g_down


def solution(mesh):
    fine = Mesh(mesh.devices.reshape(2, 4, 2, 4, 2), ("yh", "x", "yl", "z", "core"))
    tokens = P(("yh", "x", "yl", "z", "core"), None)
    units = ("yl", "z", "core")
    groups = ("yh", "x")
    return jax.shard_map(
        on_device,
        mesh=fine,
        in_specs=(tokens, tokens, P(None, units), P(None, units), P(units, None)),
        out_specs=(tokens, P(groups, units), P(groups, units), P(units, groups)),
        check_vma=False,
    )
```

```python
import functools

import jax
import jax.numpy as jnp
from jax import lax
from jax.experimental import pallas as pl
from jax.experimental.pallas import tpu as pltpu
from jax.sharding import Mesh, PartitionSpec as P

D = 4096
FF = 924
TILE = 256
N_TILES = 4
LAST = 160
UNITS = (TILE, TILE, TILE, LAST)
BF = jnp.bfloat16
F32 = jnp.float32
MIB = 1024 * 1024
ANY = pl.BlockSpec(memory_space=pl.ANY)
COST = 8


ORDER = (((0, 0), (0, 1), (0, 3), (1, 0)), ((0, 2), (1, 2), (1, 1), (1, 3)))
SOURCES = (0, 3, 1, 2)
SLOT = {step: (b, k) for b in range(2) for k, step in enumerate(ORDER[b])}


def ring(n, step):
    return [(i, (i + step) % n) for i in range(n)]


def send_x(a, step):
    return lax.ppermute(a, "x", ring(4, step))


def send_z(a, step):
    return lax.ppermute(a, "z", ring(4, step))


def swap(a, axis):
    return lax.ppermute(a, axis, [(0, 1), (1, 0)])


def dot(a, b, ca, cb):
    return lax.dot_general(a, b, (((ca,), (cb,)), ((), ())), preferred_element_type=F32)


def hidden_kernel(places, outs, *refs):
    n = len(outs)
    pieces, (wg_ref, wu_ref, wd_ref), dt_refs, (dn_ref, tok, sems) = (
        refs[: -6 - n],
        refs[-6 - n : -3 - n],
        refs[-3 - n : -3],
        refs[-3:],
    )
    j = pl.program_id(0)

    @pl.when(j == 0)
    def _():
        copies = []

        def put(src, dst):
            copies.append(pltpu.make_async_copy(src, dst, sems.at[len(copies)]))

        for c in range(2):
            for i, place in enumerate(places):
                ref = pieces[len(places) * c + i]
                for part, (array, k) in enumerate(place):
                    dst = pl.ds(128 * c + 32 * k, 32)
                    if array is None:
                        put(ref, tok.at[:, dst, :])
                    else:
                        put(ref.at[part], tok.at[array, dst, :])
        for copy in copies:
            copy.start()
        for copy in copies:
            copy.wait()

    gate = dot(wg_ref[...], tok[0], 1, 1)
    up = dot(wu_ref[...], tok[0], 1, 1)
    d_hidden = dot(wd_ref[...], tok[1], 1, 1)
    sig = 1.0 / (1.0 + jnp.exp(-gate))
    act = gate * sig
    hidden = (act * up).astype(BF)
    d_up = (d_hidden * act).astype(BF)
    d_gate = (d_hidden * up * sig * (1.0 + gate * (1.0 - sig))).astype(BF)
    dn_ref[0] = d_gate.T
    dn_ref[1] = d_up.T

    for dt_ref, tiles in zip(dt_refs, outs):
        for i, tile in enumerate(tiles):

            @pl.when(j == tile)
            def _():
                n = UNITS[tile]
                for part, value in enumerate((d_gate, d_up, hidden)):
                    row = 3 * TILE * i + n * part
                    dt_ref[row : row + n] = value[:n]


def hidden_call(pieces, places, outs, wg_rows, wu_rows, w_down):
    rows = [sum(3 * UNITS[t] for t in tiles) for tiles in outs]
    weight = pl.BlockSpec((TILE, D), lambda j: (j, 0))
    return pl.pallas_call(
        functools.partial(hidden_kernel, places, outs),
        grid=(N_TILES,),
        in_specs=[ANY] * len(pieces) + [weight] * 3,
        out_specs=[
            *[pl.BlockSpec((r, 256), lambda j: (0, 0)) for r in rows],
            pl.BlockSpec((2, 256, TILE), lambda j: (0, 0, j)),
        ],
        out_shape=[
            *[jax.ShapeDtypeStruct((r, 256), BF) for r in rows],
            jax.ShapeDtypeStruct((2, 256, FF), BF),
        ],
        scratch_shapes=[pltpu.VMEM((2, 256, D), BF), pltpu.SemaphoreType.DMA((16,))],
        compiler_params=pltpu.CompilerParams(vmem_limit_bytes=48 * MIB),
        cost_estimate=pl.CostEstimate(
            flops=6 * 256 * D * FF // COST, bytes_accessed=6 * D * FF // COST, transcendentals=0
        ),
        name="hidden_grads",
    )(*pieces, wg_rows, wu_rows, w_down)


def in_grads_kernel(pos_ref, dn0_ref, dn1_ref, wg_ref, wu_ref, own_ref, other_ref, dn):
    @pl.when(pl.program_id(0) == 0)
    def _():
        for a in range(2):
            dn[a, :256, :] = dn0_ref[a]
            dn[a, 256:, :] = dn1_ref[a]

    p = (dot(dn[0], wg_ref[...], 1, 0) + dot(dn[1], wu_ref[...], 1, 0)).astype(BF)
    yl, z = pos_ref[0], pos_ref[1]
    for b in range(2):
        for c, out_ref in enumerate((own_ref, other_ref)):
            for i, (y_step, z_step) in enumerate(ORDER[b]):
                row = 256 * b + 128 * c + 32 * i
                out_ref[lax.rem(z_step + z, 4), y_step ^ yl] = p[row : row + 32]


def in_grads_call(pos, dn0, dn1, wg_rows, wu_rows):
    cols = 512
    whole = pl.BlockSpec((2, 256, FF), lambda j, p: (0, 0, 0))
    weight = pl.BlockSpec((FF, cols), lambda j, p: (0, j))
    out = pl.BlockSpec((4, 2, 32, cols), lambda j, p: (0, 0, 0, j))
    return pl.pallas_call(
        in_grads_kernel,
        grid_spec=pltpu.PrefetchScalarGridSpec(
            num_scalar_prefetch=1,
            grid=(D // cols,),
            in_specs=[whole, whole, weight, weight],
            out_specs=[out, out],
            scratch_shapes=[pltpu.VMEM((2, 512, FF), BF)],
        ),
        out_shape=[jax.ShapeDtypeStruct((4, 2, 32, D), BF)] * 2,
        compiler_params=pltpu.CompilerParams(vmem_limit_bytes=48 * MIB),
        cost_estimate=pl.CostEstimate(
            flops=4 * 512 * D * FF // COST, bytes_accessed=4 * D * FF // COST, transcendentals=0
        ),
        name="in_grads_terms",
    )(pos, dn0, dn1, wg_rows, wu_rows)


def weights_kernel(n, places, pos_ref, *refs):
    pieces, col_pieces = refs[:5], refs[5:15]
    send_ref, keep_ref, stack, x, sems = refs[15:]
    start, stride, second = places
    sources = []
    for step in SOURCES:
        first = lax.rem(pos_ref[2] + step, 4) * stride + start
        sources.append(pieces[0].at[pl.ds(pl.multiple_of(first, 32), 3 * n), :])
    sources += [ref.at[pl.ds(second, 3 * n), :] for ref in pieces[1:4]]
    sources.append(pieces[4])
    halves = ([], [])
    count = [0]

    def put(group, src, dst):
        copy = pltpu.make_async_copy(src, dst, sems.at[count[0]])
        count[0] += 1
        copy.start()
        group.append(copy)

    for b in range(2):
        for s in range(4):
            i = 4 * b + s
            put(halves[0], sources[i], stack.at[b, :, pl.ds(256 * s, 256)])
    for h in range(2):
        cols = pl.ds(512 * h, 512)
        for c in range(2):
            here, left, far_in, far_grad, right = col_pieces[5 * c : 5 * c + 5]
            for y in range(2):
                for z, ref in ((0, here), (1, left), (3, right)):
                    b, k = SLOT[y, z]
                    put(halves[h], ref.at[y, :, :, :, cols], x.at[b, :, :, c, k, :, cols])
                b, k = SLOT[y, 2]
                put(halves[h], far_in.at[y, :, :, cols], x.at[b, 0, :, c, k, :, cols])
                put(halves[h], far_grad.at[y, :, :, cols], x.at[b, 1, :, c, k, :, cols])

    for h, out_ref in enumerate((send_ref, keep_ref)):
        for copy in halves[h]:
            copy.wait()

        def total(rows, a):
            parts = [
                dot(stack[b, rows, :], x[b, a, :, :, :, :, 512 * h : 512 * h + 512].reshape(1024, 512), 1, 0)
                for b in range(2)
            ]
            return (parts[0] + parts[1]).astype(BF)

        out_ref[: 2 * n] = total(slice(0, 2 * n), 0)
        out_ref[2 * n :] = total(slice(2 * n, 3 * n), 1)


def weights_call(n, pos, places, pieces, col_pieces):
    return pl.pallas_call(
        functools.partial(weights_kernel, n, places),
        in_specs=[pl.BlockSpec(memory_space=pltpu.SMEM)] + [ANY] * 15,
        out_specs=[pl.BlockSpec(memory_space=pltpu.VMEM)] * 2,
        out_shape=[jax.ShapeDtypeStruct((3 * n, 512), BF)] * 2,
        scratch_shapes=[
            pltpu.VMEM((2, 3 * n, 1024), BF),
            pltpu.VMEM((2, 2, 4, 2, 4, 32, 1024), BF),
            pltpu.SemaphoreType.DMA((48,)),
        ],
        compiler_params=pltpu.CompilerParams(vmem_limit_bytes=48 * MIB),
        cost_estimate=pl.CostEstimate(
            flops=6 * n * 2048 * 1024 // COST, bytes_accessed=(12 << 20) // COST, transcendentals=0
        ),
        name="weight_grads",
    )(pos, *pieces, *col_pieces)


def gate(*arrays):
    return lax.optimization_barrier(arrays)


def core_swaps(pieces):
    return [swap(p, "core") for p in pieces]


def on_device(inputs, out_grads, w_gate, w_up, w_down):
    xi, yh, yl, zi = (lax.axis_index(a) for a in ("x", "yh", "yl", "z"))
    pos = jnp.stack([yl, zi, xi]).astype(jnp.int32)
    wg_rows, wu_rows = w_gate.T, w_up.T
    mine = jnp.stack([inputs, out_grads])

    def block_for(step):
        group = lax.rem(xi + step, 4)
        starts = [((1 - yh) * 4 + group) * 512, (yh * 4 + group) * 512]
        return jnp.concatenate([lax.dynamic_slice_in_dim(mine, s, 512, axis=2) for s in starts], axis=2)

    right, left = send_z(mine, 1), send_z(mine, -1)
    partner = swap(mine, "yl")
    from_x = [block_for(0), send_x(block_for(1), 1), send_x(block_for(3), -1), send_x(block_for(2), 2)]
    right, left, partner, *from_x = gate(right, left, partner, *from_x)

    shares = jnp.stack(from_x, axis=1)
    other_shares = swap(shares, "yl")
    p_right, p_left = send_z(partner, 1), send_z(partner, -1)
    batch0 = [mine, left, right, partner]
    batch0 += core_swaps(batch0)
    both = ((None, 0),), ((None, 1),), ((None, 2),), ((None, 3),)
    *own0, dn0 = hidden_call(batch0, both, ((0, 1), (2, 3)), wg_rows, wu_rows, w_down)
    *own0, dn0, p_right, p_left, shares, other_shares = gate(*own0, dn0, p_right, p_left, shares, other_shares)
    gathered0 = [lax.all_gather(own0[0], "x", axis=0, tiled=True)]

    far_in = send_z(jnp.stack([right[0], p_right[0]]), 1)
    far_grad = send_z(jnp.stack([left[1], p_left[1]]), -1)
    batch1 = [far_in, far_grad, p_left, p_right]
    batch1 += core_swaps(batch1)
    shares = jnp.stack([shares, other_shares])
    shares, *batch1 = gate(shares, *batch1)

    places = ((0, 0), (0, 1)), ((1, 0), (1, 1)), ((None, 2),), ((None, 3),)
    *own1, dn1 = hidden_call(batch1, places, ((0, 1), (2, 3)), wg_rows, wu_rows, w_down)
    c_right, c_left = send_z(shares, 1), send_z(shares, -1)
    right1, left1 = [send_x(own1[0], 1)], [send_x(own1[0], -1)]
    cut = 3 * TILE
    c_far_in, c_far_grad = send_z(c_right[:, 0], 1), send_z(c_left[:, 1], -1)
    shares_other = swap(shares, "core")
    term_own, term_other = in_grads_call(pos, dn0, dn1, wg_rows, wu_rows)
    term_own, term_other, c_far_in, c_far_grad, right1[0], left1[0], own1[1], shares_other, c_left, c_right, gathered0[0] = gate(
        term_own, term_other, c_far_in, c_far_grad, right1[0], left1[0], own1[1], shares_other, c_left, c_right, gathered0[0]
    )

    far1 = [send_x(right1[0][:cut], 1), send_x(left1[0][cut:], -1)]
    c_here = [c_left, c_far_in, c_far_grad, c_right]
    c_other = core_swaps(c_here)
    term_other = swap(term_other, "core")
    *far1, own1[1], own0[1], term_other = gate(*far1, own1[1], own0[1], term_other, *c_other)[:5]
    gathered0.append(lax.all_gather(own0[1], "x", axis=0, tiled=True))
    col_pieces = [shares, *c_here, shares_other, *c_other]
    kept, sent, got = [], [], []

    def weights(j):
        side, start = j // 2, cut * (j % 2)
        pieces = [gathered0[side], own1[side], right1[side], left1[side], far1[j]]
        send, keep = weights_call(UNITS[j], pos, (start, own0[side].shape[0], start), pieces, col_pieces)
        kept.append(keep)
        sent.append(send)

    right1.append(send_x(own1[1], 1))
    left1.append(send_x(own1[1], -1))
    weights(0)
    sent[0], own1[0] = gate(sent[0], own1[0])
    got.append(swap(sent[0], "yh"))
    weights(1)
    pair = (term_own.astype(F32) + term_other.astype(F32)).astype(BF)
    right1[1], left1[1], _, gathered0[1], pair, got[0] = gate(
        right1[1], left1[1], sent[1], gathered0[1], pair, got[0]
    )
    scattered = lax.psum_scatter(pair.reshape(256, D), "z", scatter_dimension=0, tiled=True)
    got.append(swap(sent[1], "yh"))
    far1 += [send_x(right1[1][:cut], 1), send_x(left1[1][cut:], -1)]
    scattered = scattered.reshape(2, 32, D)
    mine_part = lax.dynamic_index_in_dim(scattered, yl, axis=0, keepdims=False)
    other_part = lax.dynamic_index_in_dim(scattered, 1 - yl, axis=0, keepdims=False)
    in_grads = (mine_part.astype(F32) + swap(other_part, "yl").astype(F32)).astype(BF)
    far1[2], far1[3], got[1], own1[1] = gate(far1[2], far1[3], got[1], own1[1])
    weights(2)
    got.append(swap(sent[2], "yh"))
    sent[2], own1[1] = gate(sent[2], own1[1])
    weights(3)
    got.append(swap(sent[3], "yh"))
    sent = got

    gate_parts, up_parts, down_parts = [], [], []
    for j in range(N_TILES):
        n = TILE if j < N_TILES - 1 else LAST
        used = min(n, FF - TILE * j)
        total = (kept[j].astype(F32) + sent[j].astype(F32)).astype(BF)
        gate_parts.append(total[:used])
        up_parts.append(total[n : n + used])
        down_parts.append(total[2 * n : 2 * n + used])
    g_gate = jnp.concatenate(gate_parts, axis=0).T
    g_up = jnp.concatenate(up_parts, axis=0).T
    g_down = jnp.concatenate(down_parts, axis=0)
    return in_grads, g_gate, g_up, g_down


def solution(mesh):
    fine = Mesh(mesh.devices.reshape(2, 4, 2, 4, 2), ("yh", "x", "yl", "z", "core"))
    tokens = P(("yh", "x", "yl", "z", "core"), None)
    units = ("yl", "z", "core")
    groups = ("yh", "x")
    return jax.shard_map(
        on_device,
        mesh=fine,
        in_specs=(tokens, tokens, P(None, units), P(None, units), P(units, None)),
        out_specs=(tokens, P(groups, units), P(groups, units), P(units, groups)),
        check_vma=False,
    )
```

```python
import functools

import jax
import jax.numpy as jnp
from jax import lax
from jax.experimental import pallas as pl
from jax.experimental.pallas import tpu as pltpu
from jax.sharding import Mesh, PartitionSpec as P

D = 4096
FF = 924
TILE = 256
N_TILES = 4
LAST = 160
UNITS = (TILE, TILE, TILE, LAST)
BF = jnp.bfloat16
F32 = jnp.float32
MIB = 1024 * 1024
ANY = pl.BlockSpec(memory_space=pl.ANY)
COST = 8


ORDER = (((0, 0), (0, 1), (0, 3), (1, 0)), ((0, 2), (1, 2), (1, 1), (1, 3)))
SOURCES = (0, 3, 1, 2)
SLOT = {step: (b, k) for b in range(2) for k, step in enumerate(ORDER[b])}


def ring(n, step):
    return [(i, (i + step) % n) for i in range(n)]


def send_x(a, step):
    return lax.ppermute(a, "x", ring(4, step))


def send_z(a, step):
    return lax.ppermute(a, "z", ring(4, step))


def swap(a, axis):
    return lax.ppermute(a, axis, [(0, 1), (1, 0)])


def dot(a, b, ca, cb):
    return lax.dot_general(a, b, (((ca,), (cb,)), ((), ())), preferred_element_type=F32)


def hidden_kernel(places, outs, *refs):
    n = len(outs)
    pieces, (wg_ref, wu_ref, wd_ref), dt_refs, (dn_ref, tok, sems) = (
        refs[: -6 - n],
        refs[-6 - n : -3 - n],
        refs[-3 - n : -3],
        refs[-3:],
    )
    j = pl.program_id(0)

    @pl.when(j == 0)
    def _():
        copies = []

        def put(src, dst):
            copies.append(pltpu.make_async_copy(src, dst, sems.at[len(copies)]))

        for c in range(2):
            for i, place in enumerate(places):
                ref = pieces[len(places) * c + i]
                for part, (array, k) in enumerate(place):
                    dst = pl.ds(128 * c + 32 * k, 32)
                    if array is None:
                        put(ref, tok.at[:, dst, :])
                    else:
                        put(ref.at[part], tok.at[array, dst, :])
        for copy in copies:
            copy.start()
        for copy in copies:
            copy.wait()

    gate = dot(wg_ref[...], tok[0], 1, 1)
    up = dot(wu_ref[...], tok[0], 1, 1)
    d_hidden = dot(wd_ref[...], tok[1], 1, 1)
    sig = 1.0 / (1.0 + jnp.exp(-gate))
    act = gate * sig
    hidden = (act * up).astype(BF)
    d_up = (d_hidden * act).astype(BF)
    d_gate = (d_hidden * up * sig * (1.0 + gate * (1.0 - sig))).astype(BF)
    dn_ref[0] = d_gate.T
    dn_ref[1] = d_up.T

    for dt_ref, tiles in zip(dt_refs, outs):
        for i, tile in enumerate(tiles):

            @pl.when(j == tile)
            def _():
                n = UNITS[tile]
                for part, value in enumerate((d_gate, d_up, hidden)):
                    row = 3 * TILE * i + n * part
                    dt_ref[row : row + n] = value[:n]


def hidden_call(pieces, places, outs, wg_rows, wu_rows, w_down):
    rows = [sum(3 * UNITS[t] for t in tiles) for tiles in outs]
    weight = pl.BlockSpec((TILE, D), lambda j: (j, 0))
    return pl.pallas_call(
        functools.partial(hidden_kernel, places, outs),
        grid=(N_TILES,),
        in_specs=[ANY] * len(pieces) + [weight] * 3,
        out_specs=[
            *[pl.BlockSpec((r, 256), lambda j: (0, 0)) for r in rows],
            pl.BlockSpec((2, 256, TILE), lambda j: (0, 0, j)),
        ],
        out_shape=[
            *[jax.ShapeDtypeStruct((r, 256), BF) for r in rows],
            jax.ShapeDtypeStruct((2, 256, FF), BF),
        ],
        scratch_shapes=[pltpu.VMEM((2, 256, D), BF), pltpu.SemaphoreType.DMA((16,))],
        compiler_params=pltpu.CompilerParams(vmem_limit_bytes=48 * MIB),
        cost_estimate=pl.CostEstimate(
            flops=6 * 256 * D * FF // COST, bytes_accessed=6 * D * FF // COST, transcendentals=0
        ),
        name="hidden_grads",
    )(*pieces, wg_rows, wu_rows, w_down)


def in_grads_kernel(pos_ref, dn0_ref, dn1_ref, wg_ref, wu_ref, own_ref, other_ref, dn):
    @pl.when(pl.program_id(0) == 0)
    def _():
        for a in range(2):
            dn[a, :256, :] = dn0_ref[a]
            dn[a, 256:, :] = dn1_ref[a]

    p = (dot(dn[0], wg_ref[...], 1, 0) + dot(dn[1], wu_ref[...], 1, 0)).astype(BF)
    yl, z = pos_ref[0], pos_ref[1]
    for b in range(2):
        for c, out_ref in enumerate((own_ref, other_ref)):
            for i, (y_step, z_step) in enumerate(ORDER[b]):
                row = 256 * b + 128 * c + 32 * i
                out_ref[lax.rem(z_step + z, 4), y_step ^ yl] = p[row : row + 32]


def in_grads_call(pos, dn0, dn1, wg_rows, wu_rows):
    cols = 512
    whole = pl.BlockSpec((2, 256, FF), lambda j, p: (0, 0, 0))
    weight = pl.BlockSpec((FF, cols), lambda j, p: (0, j))
    out = pl.BlockSpec((4, 2, 32, cols), lambda j, p: (0, 0, 0, j))
    return pl.pallas_call(
        in_grads_kernel,
        grid_spec=pltpu.PrefetchScalarGridSpec(
            num_scalar_prefetch=1,
            grid=(D // cols,),
            in_specs=[whole, whole, weight, weight],
            out_specs=[out, out],
            scratch_shapes=[pltpu.VMEM((2, 512, FF), BF)],
        ),
        out_shape=[jax.ShapeDtypeStruct((4, 2, 32, D), BF)] * 2,
        compiler_params=pltpu.CompilerParams(vmem_limit_bytes=48 * MIB),
        cost_estimate=pl.CostEstimate(
            flops=4 * 512 * D * FF // COST, bytes_accessed=4 * D * FF // COST, transcendentals=0
        ),
        name="in_grads_terms",
    )(pos, dn0, dn1, wg_rows, wu_rows)


def weights_kernel(n, places, pos_ref, *refs):
    pieces, col_pieces = refs[:5], refs[5:15]
    send_ref, keep_ref, stack, x, sems = refs[15:]
    start, stride, second = places
    sources = []
    for step in SOURCES:
        first = lax.rem(pos_ref[2] + step, 4) * stride + start
        sources.append(pieces[0].at[pl.ds(pl.multiple_of(first, 32), 3 * n), :])
    sources += [ref.at[pl.ds(second, 3 * n), :] for ref in pieces[1:4]]
    sources.append(pieces[4])
    halves = ([], [])
    count = [0]

    def put(group, src, dst):
        copy = pltpu.make_async_copy(src, dst, sems.at[count[0]])
        count[0] += 1
        copy.start()
        group.append(copy)

    for b in range(2):
        for s in range(4):
            i = 4 * b + s
            put(halves[0], sources[i], stack.at[b, :, pl.ds(256 * s, 256)])
    for h in range(2):
        cols = pl.ds(512 * h, 512)
        for c in range(2):
            here, left, far_in, far_grad, right = col_pieces[5 * c : 5 * c + 5]
            for y in range(2):
                for z, ref in ((0, here), (1, left), (3, right)):
                    b, k = SLOT[y, z]
                    put(halves[h], ref.at[y, :, :, :, cols], x.at[b, :, :, c, k, :, cols])
                b, k = SLOT[y, 2]
                put(halves[h], far_in.at[y, :, :, cols], x.at[b, 0, :, c, k, :, cols])
                put(halves[h], far_grad.at[y, :, :, cols], x.at[b, 1, :, c, k, :, cols])

    for h, out_ref in enumerate((send_ref, keep_ref)):
        for copy in halves[h]:
            copy.wait()

        def total(rows, a):
            parts = [
                dot(stack[b, rows, :], x[b, a, :, :, :, :, 512 * h : 512 * h + 512].reshape(1024, 512), 1, 0)
                for b in range(2)
            ]
            return (parts[0] + parts[1]).astype(BF)

        out_ref[: 2 * n] = total(slice(0, 2 * n), 0)
        out_ref[2 * n :] = total(slice(2 * n, 3 * n), 1)


def weights_call(n, pos, places, pieces, col_pieces):
    return pl.pallas_call(
        functools.partial(weights_kernel, n, places),
        in_specs=[pl.BlockSpec(memory_space=pltpu.SMEM)] + [ANY] * 15,
        out_specs=[pl.BlockSpec(memory_space=pltpu.VMEM)] * 2,
        out_shape=[jax.ShapeDtypeStruct((3 * n, 512), BF)] * 2,
        scratch_shapes=[
            pltpu.VMEM((2, 3 * n, 1024), BF),
            pltpu.VMEM((2, 2, 4, 2, 4, 32, 1024), BF),
            pltpu.SemaphoreType.DMA((48,)),
        ],
        compiler_params=pltpu.CompilerParams(vmem_limit_bytes=48 * MIB),
        cost_estimate=pl.CostEstimate(
            flops=6 * n * 2048 * 1024, bytes_accessed=12 << 20, transcendentals=0
        ),
        name="weight_grads",
    )(pos, *pieces, *col_pieces)


def gate(*arrays):
    return lax.optimization_barrier(arrays)


def core_swaps(pieces):
    return [swap(p, "core") for p in pieces]


def on_device(inputs, out_grads, w_gate, w_up, w_down):
    xi, yh, yl, zi = (lax.axis_index(a) for a in ("x", "yh", "yl", "z"))
    pos = jnp.stack([yl, zi, xi]).astype(jnp.int32)
    wg_rows, wu_rows = w_gate.T, w_up.T
    mine = jnp.stack([inputs, out_grads])

    def block_for(step):
        group = lax.rem(xi + step, 4)
        starts = [((1 - yh) * 4 + group) * 512, (yh * 4 + group) * 512]
        return jnp.concatenate([lax.dynamic_slice_in_dim(mine, s, 512, axis=2) for s in starts], axis=2)

    right, left = send_z(mine, 1), send_z(mine, -1)
    partner = swap(mine, "yl")
    from_x = [block_for(0), send_x(block_for(1), 1), send_x(block_for(3), -1), send_x(block_for(2), 2)]
    right, left, partner, *from_x = gate(right, left, partner, *from_x)

    shares = jnp.stack(from_x, axis=1)
    other_shares = swap(shares, "yl")
    p_right, p_left = send_z(partner, 1), send_z(partner, -1)
    batch0 = [mine, left, right, partner]
    batch0 += core_swaps(batch0)
    both = ((None, 0),), ((None, 1),), ((None, 2),), ((None, 3),)
    own0, dn0 = hidden_call(batch0, both, ((0, 1, 2, 3),), wg_rows, wu_rows, w_down)
    own0, dn0, p_right, p_left, shares, other_shares = gate(own0, dn0, p_right, p_left, shares, other_shares)
    gathered0 = lax.all_gather(own0, "x", axis=0, tiled=True)

    far_in = send_z(jnp.stack([right[0], p_right[0]]), 1)
    far_grad = send_z(jnp.stack([left[1], p_left[1]]), -1)
    batch1 = [far_in, far_grad, p_left, p_right]
    batch1 += core_swaps(batch1)
    shares = jnp.stack([shares, other_shares])
    shares, *batch1 = gate(shares, *batch1)

    places = ((0, 0), (0, 1)), ((1, 0), (1, 1)), ((None, 2),), ((None, 3),)
    *own1, dn1 = hidden_call(batch1, places, ((0, 1), (2, 3)), wg_rows, wu_rows, w_down)
    c_right, c_left = send_z(shares, 1), send_z(shares, -1)
    right1, left1 = [send_x(own1[0], 1)], [send_x(own1[0], -1)]
    cut = 3 * TILE
    c_far_in, c_far_grad = send_z(c_right[:, 0], 1), send_z(c_left[:, 1], -1)
    shares_other = swap(shares, "core")
    term_own, term_other = in_grads_call(pos, dn0, dn1, wg_rows, wu_rows)
    term_own, term_other, c_far_in, c_far_grad, right1[0], left1[0], own1[1], shares_other, c_left, c_right, gathered0 = gate(
        term_own, term_other, c_far_in, c_far_grad, right1[0], left1[0], own1[1], shares_other, c_left, c_right, gathered0
    )

    far1 = [send_x(right1[0][:cut], 1), send_x(left1[0][cut:], -1)]
    c_here = [c_left, c_far_in, c_far_grad, c_right]
    c_other = core_swaps(c_here)
    term_other = swap(term_other, "core")
    *far1, own1[1], term_other = gate(*far1, own1[1], term_other, *c_other)[:4]
    col_pieces = [shares, *c_here, shares_other, *c_other]
    kept, sent, got = [], [], []

    def weights(j):
        side, start = j // 2, cut * (j % 2)
        pieces = [gathered0, own1[side], right1[side], left1[side], far1[j]]
        send, keep = weights_call(UNITS[j], pos, (cut * j, own0.shape[0], start), pieces, col_pieces)
        kept.append(keep)
        sent.append(send)

    right1.append(send_x(own1[1], 1))
    left1.append(send_x(own1[1], -1))
    weights(0)
    sent[0], own1[0], term_other = gate(sent[0], own1[0], term_other)
    pair = (term_own.astype(F32) + term_other.astype(F32)).astype(BF)
    scattered = lax.psum_scatter(pair.reshape(256, D), "z", scatter_dimension=0, tiled=True)
    got.append(swap(sent[0], "yh"))
    weights(1)
    right1[1], left1[1], sent[1] = gate(right1[1], left1[1], sent[1])
    got.append(swap(sent[1], "yh"))
    far1 += [send_x(right1[1][:cut], 1), send_x(left1[1][cut:], -1)]
    scattered = scattered.reshape(2, 32, D)
    mine_part = lax.dynamic_index_in_dim(scattered, yl, axis=0, keepdims=False)
    other_part = lax.dynamic_index_in_dim(scattered, 1 - yl, axis=0, keepdims=False)
    in_grads = (mine_part.astype(F32) + swap(other_part, "yl").astype(F32)).astype(BF)
    far1[2], far1[3], got[0], own1[1] = gate(far1[2], far1[3], got[0], own1[1])
    weights(2)
    got.append(swap(sent[2], "yh"))
    got[1], sent[2], own1[1] = gate(got[1], sent[2], own1[1])
    weights(3)
    got.append(swap(sent[3], "yh"))
    sent = got

    gate_parts, up_parts, down_parts = [], [], []
    for j in range(N_TILES):
        n = TILE if j < N_TILES - 1 else LAST
        used = min(n, FF - TILE * j)
        total = (kept[j].astype(F32) + sent[j].astype(F32)).astype(BF)
        gate_parts.append(total[:used])
        up_parts.append(total[n : n + used])
        down_parts.append(total[2 * n : 2 * n + used])
    g_gate = jnp.concatenate(gate_parts, axis=0).T
    g_up = jnp.concatenate(up_parts, axis=0).T
    g_down = jnp.concatenate(down_parts, axis=0)
    return in_grads, g_gate, g_up, g_down


def solution(mesh):
    fine = Mesh(mesh.devices.reshape(2, 4, 2, 4, 2), ("yh", "x", "yl", "z", "core"))
    tokens = P(("yh", "x", "yl", "z", "core"), None)
    units = ("yl", "z", "core")
    groups = ("yh", "x")
    return jax.shard_map(
        on_device,
        mesh=fine,
        in_specs=(tokens, tokens, P(None, units), P(None, units), P(units, None)),
        out_specs=(tokens, P(groups, units), P(groups, units), P(units, groups)),
        check_vma=False,
    )
```
